32 devices in a mesh: groups: 2 (over y), chan: 4 (over z), win: 4 (over x, core).
Axes of the slice: x: 2, y: 2, z: 4, core: 2. Of those that a mesh axis runs over, the one named last changes fastest.
Arguments:
- tokens: bfloat16 [8, 1024, 512], P(('groups', 'win'), 'chan'), parts along dimension 0, may hold values from -6 to 6
- head_weight: bfloat16 [512, 1024], replicated, may hold values from -0.25 to 0.25
- target: bfloat16 [8, 512, 2048], P(('groups', 'win'), 'chan'), parts along dimension 0, may hold values from -6 to 6
- target_amp: bfloat16 [8, 512, 2048], P(('groups', 'win'), 'chan'), parts along dimension 0, may hold values from 0.29882812 to 3
- patch_ranks: int32 [8, 1024], P(('groups', 'win'), 'chan'), parts along dimension 0, may hold values from 0 to 1023, each once within a row
Outputs:
- grad_tokens: bfloat16 [8, 1024, 512], P(('groups', 'win'), 'chan'), parts along dimension 0
- grad_weight: float32 [1024, 1024], P(('groups', 'chan'), 'win'), parts along dimension 0
The draws below stay inside these ranges and needn't reach their ends.
There are 2 independent parts, one for each index of `groups`. The reference program is written for one: setup_inputs(seed, part) draws one part's arguments, and reference() takes and returns one part's arrays. A program takes and returns all parts, laid end to end along the dimension named above; an argument that names none is the same for every part. Nothing has to cross between parts.
Inputs may be any that keep to these rules, and one draw needn't show every extreme that they name: `patch_ranks`: each window's row is a permutation of 0 to 1023; a patch is masked exactly when its rank is 256 or more.
All inputs are finite; a program needn't handle non-finite values.
Results may differ from the reference program's by a relative error of at most 0.0052.
Values sent between devices are 32-bit elements; how exact they have to be, the bound alone decides.
A program may use at most 128 MiB of HBM per device.

```python
import math
import jax
import jax.numpy as jnp
from jax import lax

E = 512
PATCH_C = 16
PATCH_S = 64
S = 2048
C = 512
W = 4
PIX = 1024
PCH = 32
PSN = 32
P_SIZE = 1024
KEEP = 256


def spiked(array, stream_key, source, target, parts, factor):
    def block_of(dim):
        return (jnp.arange(array.shape[dim]) // (array.shape[dim] // parts)).reshape((-1,) + (1,) * (array.ndim - 1 - dim))

    near = jax.random.permutation(stream_key, parts)[block_of(target)]
    second = (block_of(target) + parts // 2) % parts
    return jnp.where((block_of(source) == near) | (block_of(source) == second), factor * array, array)


def steps_of(key, extent, cuts, least, high):
    level, own = 1.0, jax.random.fold_in(key, 6)
    for axis_at, shards_of in cuts:
        heights = jnp.exp(jax.random.uniform(jax.random.fold_in(own, axis_at), (shards_of,), jnp.float32, least / len(cuts), high / len(cuts)))
        level = level * jnp.repeat(heights, extent[axis_at] // shards_of).reshape([-1 if axis == axis_at else 1 for axis in range(len(extent))])
    return level


def noise(key, extent, width, reach, cuts=(), held_as=jnp.bfloat16):
    loudness = steps_of(key, extent, cuts, -0.22, 0.18) if cuts else 1.0
    values = jax.random.normal(key, extent, jnp.float32) * width * loudness
    return jnp.minimum(jnp.maximum(values, -reach), reach).astype(held_as)


def bell_draw_with(key, shape, deviation, limit, pieces, heavy, held_as=jnp.bfloat16):
    array = deviation * jax.random.normal(key, shape, jnp.float32)
    if pieces:
        array = array * steps_of(key, shape, pieces, -0.22, 0.18)
    return jnp.clip(spiked(array, jax.random.fold_in(key, 3), *heavy), -limit, limit).astype(held_as)


def setup_inputs(seed: int = 0, part: int = 0) -> dict:
    key_list = jax.random.split(jax.random.key(seed), 6)
    part_keys = jax.random.split(jax.random.fold_in(key_list[5], part), 6)
    tokens = bell_draw_with(part_keys[0], (W, P_SIZE, E), 1.0, 6.0, ((0, 4), (1, 4)), (1, 2, 4, 2.0))
    head_weight = noise(key_list[1], (E, PIX), E ** -0.5, 0.25)
    target = noise(part_keys[2], (W, C, S), 1.0, 6.0, ((0, 4), (1, 4)))
    target_amp = jnp.clip(jnp.exp(math.log(3.0) - 2.306499 * jax.random.uniform(part_keys[3], (W, C, S), jnp.float32) ** steps_of(part_keys[3], (W, C, S), ((0, 4), (1, 4)), -0.2, 0.2)), 0.29882812, 3.0).astype(jnp.bfloat16)
    patch_ranks = jax.vmap(lambda own: jax.random.permutation(own, P_SIZE))(jax.random.split(part_keys[4], W)).reshape((W, P_SIZE)).astype(jnp.int32)
    return {"tokens": tokens, "head_weight": head_weight, "target": target, "target_amp": target_amp, "patch_ranks": patch_ranks}


def reference(tokens, head_weight, target, target_amp, patch_ranks):

    def window_grads(carry, items):
        token_rows, target_img, amp_img, rank_row = items
        patches = jnp.dot(token_rows, head_weight, preferred_element_type=jnp.float32).astype(jnp.bfloat16)
        image = patches.reshape(PCH, PSN, PATCH_C, PATCH_S).transpose(0, 2, 1, 3).reshape(C, S)
        masked = (rank_row >= KEEP).reshape(PCH, 1, PSN, 1)
        pixel_mask = jnp.broadcast_to(masked, (PCH, PATCH_C, PSN, PATCH_S)).reshape(C, S)
        composite = jnp.where(pixel_mask, image, target_img)
        spectrum = jnp.fft.fft2(composite.astype(jnp.float32), norm='ortho')
        real_part = spectrum.real
        imag_part = spectrum.imag
        amplitude = jnp.sqrt(real_part * real_part + imag_part * imag_part + 1.0)
        weighting = (amplitude - amp_img.astype(jnp.float32)) / (amplitude * W)
        grad_image = jnp.fft.ifft2(weighting * spectrum, norm='ortho').real
        grad_image = jnp.where(pixel_mask, grad_image, 0.0)
        grad_patches = grad_image.reshape(PCH, PATCH_C, PSN, PATCH_S).transpose(0, 2, 1, 3).reshape(P_SIZE, PIX).astype(jnp.bfloat16)
        grad_rows = jnp.dot(grad_patches, head_weight.T, preferred_element_type=jnp.float32).astype(jnp.bfloat16)
        weight_term = jnp.dot(token_rows.T, grad_patches, preferred_element_type=jnp.float32)
        return (carry + weight_term, grad_rows)
    start = jnp.zeros((E, PIX), jnp.float32)
    grad_weight, grad_tokens = lax.scan(window_grads, start, (tokens, target, target_amp, patch_ranks))
    return (grad_tokens, grad_weight)
```

```python
from functools import partial
import math

import jax
import jax.numpy as jnp
import numpy as np
from jax import lax
from jax.sharding import PartitionSpec as P

PATCH_C = 16
PATCH_S = 64
DENSE_LIMIT = 1024
F32 = jnp.float32
BF16 = jnp.bfloat16

product = partial(jnp.einsum, precision=lax.Precision.HIGHEST)


def two_parts(table):
    high = table.astype(BF16)
    low = (table - high.astype(np.float64)).astype(BF16)
    return high, low


def time_table(samples, blocks):
    half = samples // 2
    freq = np.arange(half)[:, None] * np.arange(samples)[None, :] % samples
    angles = 2.0 * np.pi / samples * freq
    cosine = np.cos(angles)
    sine = -np.sin(angles)
    sine[0] = 1.0 - 2.0 * (np.arange(samples) % 2)
    both = np.stack([cosine.reshape(blocks, -1, samples), sine.reshape(blocks, -1, samples)], axis=1)
    return both.reshape(samples, samples)


def chan_table(channels, blocks):
    angles = 2.0 * np.pi / channels * (np.arange(channels)[:, None] * np.arange(channels)[None, :] % channels)
    cosine = np.cos(angles)
    sine = np.sin(angles)
    table = np.stack([np.stack([cosine, sine], axis=1), np.stack([-sine, cosine], axis=1)], axis=0)
    table = table.reshape(2 * channels, 2, blocks, channels // blocks).transpose(0, 2, 1, 3)
    return table.reshape(2 * channels, 2 * channels)


def negation(length):
    table = np.zeros((length, length), np.float32)
    table[np.arange(length), -np.arange(length) % length] = 1.0
    return table.astype(BF16)


def dot(left, right, dims=((1,), (0,))):
    return lax.dot_general(left, right, (dims, ((), ())), preferred_element_type=F32)


def split(values):
    high = values.astype(BF16)
    return high, (values - high.astype(F32)).astype(BF16)


def factor_pair(length):
    first = int(math.isqrt(length))
    while length % first:
        first -= 1
    return (first, length // first)


def section_one(length, direction):
    index = jnp.arange(length, dtype=jnp.int32)
    angles = direction * 2.0 * math.pi / length * (index[:, None] * index[None, :] % length).astype(F32)
    cosine = jnp.cos(angles)
    sine = jnp.sin(angles)
    upper = jnp.stack([cosine, sine], axis=1)
    lower = jnp.stack([-sine, cosine], axis=1)
    return jnp.stack([upper, lower], axis=0)


def section_two(first, second, direction):
    length = first * second
    outer = jnp.arange(first, dtype=jnp.int32)[:, None, None]
    inner = jnp.arange(second, dtype=jnp.int32)[None, :, None]
    final = jnp.arange(second, dtype=jnp.int32)[None, None, :]
    phase = (outer * inner + first * inner * final) % length
    angles = direction * 2.0 * math.pi / length * phase.astype(F32)
    cosine = jnp.cos(angles)
    sine = jnp.sin(angles)
    upper = jnp.stack([cosine, sine], axis=2)
    lower = jnp.stack([-sine, cosine], axis=2)
    return jnp.stack([upper, lower], axis=0)


def factored_transform(spectrum, direction):
    _, length, columns = spectrum.shape
    first, second = factor_pair(length)
    shaped = spectrum.reshape(2, first, second, columns)
    section = product("rabm,rask->skbm", shaped, section_one(length=first, direction=direction))
    result = product("skbm,skbtj->tjkm", section, section_two(first, second, direction))
    return result.reshape(2, length, columns)


def chan_forward(rows, channels, blocks):
    if channels <= DENSE_LIMIT:
        table = chan_table(channels, blocks)
        high, low = two_parts(table)
        rows_high, rows_low = split(rows)
        return dot(high, rows_high) + dot(high, rows_low) + dot(low, rows_high)
    columns = rows.shape[1]
    shaped = rows.reshape(blocks, 2, channels // blocks, columns).transpose(1, 0, 2, 3)
    return factored_transform(shaped.reshape(2, channels, columns), -1.0).reshape(2 * channels, columns)


def chan_inverse(rows, channels, blocks):
    if channels <= DENSE_LIMIT:
        high, _ = two_parts(chan_table(channels, blocks))
        return dot(high, rows.astype(BF16), ((0,), (0,)))
    columns = rows.shape[1]
    shaped = factored_transform(rows.reshape(2, channels, columns), 1.0)
    shaped = shaped.reshape(2, blocks, channels // blocks, columns).transpose(1, 0, 2, 3)
    return shaped.reshape(2 * channels, columns)


def per_device(tokens, head_weight, target, target_amp, patch_ranks):
    blocks = lax.axis_size("chan")
    all_windows = lax.axis_size("win")
    tokens, target, target_amp, patch_ranks = tokens[0], target[0], target_amp[0], patch_ranks[0]
    local_patches, width = tokens.shape
    rows, samples = target.shape
    channels = rows * blocks
    half = samples // 2
    cols = half // blocks
    chan_patches = rows // PATCH_C
    sample_patches = samples // PATCH_S
    keep_count = local_patches * blocks // 4
    norm = 1.0 / math.sqrt(channels * samples)
    here = lax.axis_index("chan")

    upper = dot(target_amp[:, half:], negation(half))
    amp = jnp.stack([target_amp[:, :half].astype(F32), upper])
    amp = amp.reshape(2, rows, blocks, cols).transpose(2, 0, 1, 3)
    amp = lax.all_to_all(amp, "chan", split_axis=0, concat_axis=0, tiled=True)

    patches = dot(tokens, head_weight).astype(BF16)
    image = patches.reshape(chan_patches, sample_patches, PATCH_C, PATCH_S)
    image = image.transpose(0, 2, 1, 3).reshape(rows, samples)
    masked = (patch_ranks >= keep_count).reshape(chan_patches, 1, sample_patches, 1)
    pixel_mask = jnp.broadcast_to(masked, (chan_patches, PATCH_C, sample_patches, PATCH_S)).reshape(rows, samples)
    composite = jnp.where(pixel_mask, image, target)

    high, low = two_parts(time_table(samples, blocks))
    spectrum = dot(composite, high, ((1,), (1,))) + dot(composite, low, ((1,), (1,)))
    spectrum = spectrum.reshape(rows, blocks, 2, cols).transpose(1, 2, 0, 3)
    spectrum = lax.all_to_all(spectrum, "chan", split_axis=0, concat_axis=0, tiled=True)

    lane = lax.broadcasted_iota(jnp.int32, (1, 128), 1)
    first_col = spectrum[:, :, :, :1]
    extra = jnp.where(lane == 0, first_col[:, 0], 0.0) + jnp.where(lane == 1, first_col[:, 1], 0.0)
    extra = jnp.stack([extra, jnp.zeros_like(extra)], axis=1)
    stacked = jnp.concatenate([spectrum, extra], axis=3).reshape(2 * channels, cols + 128)
    amp_low = amp[:, 0].reshape(channels, cols)
    amp_up = amp[:, 1].reshape(channels, cols)
    amp_sum = amp_low + dot(negation(channels).astype(F32), amp_up)
    amp_extra = jnp.where(lane == 0, amp_low[:, :1], amp_up[:, :1])
    amp_all = jnp.concatenate([amp_sum, amp_extra], axis=1)

    freq = chan_forward(stacked, channels, blocks).reshape(2, channels, cols + 128) * norm
    inverse_amp = lax.rsqrt(freq[0] * freq[0] + freq[1] * freq[1] + 1.0)
    scaled = freq * (inverse_amp * amp_all * norm)
    back = chan_inverse(scaled.reshape(2 * channels, cols + 128), channels, blocks)
    back = back.reshape(blocks, 2, rows, cols + 128)
    edge = jnp.stack([back[:, 0, :, cols : cols + 1], back[:, 0, :, cols + 1 : cols + 2]], axis=1)
    column = lax.broadcasted_iota(jnp.int32, (1, 1, 1, cols), 3)
    returned = jnp.where((column == 0) & (here == 0), edge, back[:, :, :, :cols])
    returned = lax.all_to_all(returned, "chan", split_axis=0, concat_axis=0, tiled=True)

    returned = returned.transpose(2, 0, 1, 3).reshape(rows, samples)
    returned_high, returned_low = split(returned)
    pulled = dot(returned_high, high) + dot(returned_low, high)
    grad_image = jnp.where(pixel_mask, (composite.astype(F32) - pulled) * (1.0 / all_windows), 0.0)
    grad_patches = grad_image.astype(BF16).reshape(chan_patches, PATCH_C, sample_patches, PATCH_S)
    grad_patches = grad_patches.transpose(0, 2, 1, 3).reshape(local_patches, PATCH_C * PATCH_S)
    grad_tokens = dot(grad_patches, head_weight, ((1,), (1,))).astype(BF16)
    grad_weight = dot(tokens, grad_patches, ((0,), (0,)))
    grad_weight = lax.psum_scatter(grad_weight, "win", scatter_dimension=1, tiled=True)
    grad_weight = lax.psum_scatter(grad_weight, "chan", scatter_dimension=0, tiled=True)
    return (grad_tokens[None], grad_weight)


def solution(mesh):
    in_specs = (
        P(("groups", "win"), "chan", None),
        P(),
        P(("groups", "win"), "chan", None),
        P(("groups", "win"), "chan", None),
        P(("groups", "win"), "chan"),
    )
    out_specs = (P(("groups", "win"), "chan", None), P(("groups", "chan"), "win"))
    return jax.shard_map(
        per_device, mesh=mesh, in_specs=in_specs, out_specs=out_specs, check_vma=False
    )
```

```python
from functools import partial
import math

import jax
import jax.numpy as jnp
import numpy as np
from jax import lax
from jax.experimental import pallas as pl
from jax.experimental.pallas import tpu as pltpu
from jax.sharding import PartitionSpec as P

PATCH_C = 16
PATCH_S = 64
DENSE_LIMIT = 1024
F32 = jnp.float32
BF16 = jnp.bfloat16

product = partial(jnp.einsum, precision=lax.Precision.HIGHEST)


def two_parts(table):
    high = table.astype(BF16)
    low = (table - high.astype(np.float64)).astype(BF16)
    return high, low


def time_table(samples, blocks):
    half = samples // 2
    freq = np.arange(half)[:, None] * np.arange(samples)[None, :] % samples
    angles = 2.0 * np.pi / samples * freq
    cosine = np.cos(angles)
    sine = -np.sin(angles)
    sine[0] = 1.0 - 2.0 * (np.arange(samples) % 2)
    both = np.stack([cosine.reshape(blocks, -1, samples), sine.reshape(blocks, -1, samples)], axis=1)
    return both.reshape(samples, samples)


def chan_table(channels, blocks):
    angles = 2.0 * np.pi / channels * (np.arange(channels)[:, None] * np.arange(channels)[None, :] % channels)
    cosine = np.cos(angles)
    sine = np.sin(angles)
    table = np.stack([np.stack([cosine, sine], axis=1), np.stack([-sine, cosine], axis=1)], axis=0)
    table = table.reshape(2 * channels, 2, blocks, channels // blocks).transpose(0, 2, 1, 3)
    return table.reshape(2 * channels, 2 * channels)


def negation(length):
    table = np.zeros((length, length), np.float32)
    table[np.arange(length), -np.arange(length) % length] = 1.0
    return table.astype(BF16)


def dot(left, right, dims=((1,), (0,))):
    return lax.dot_general(left, right, (dims, ((), ())), preferred_element_type=F32)


def split(values):
    high = values.astype(BF16)
    return high, (values - high.astype(F32)).astype(BF16)


def factor_pair(length):
    first = int(math.isqrt(length))
    while length % first:
        first -= 1
    return (first, length // first)


def section_one(length, direction):
    index = jnp.arange(length, dtype=jnp.int32)
    angles = direction * 2.0 * math.pi / length * (index[:, None] * index[None, :] % length).astype(F32)
    cosine = jnp.cos(angles)
    sine = jnp.sin(angles)
    upper = jnp.stack([cosine, sine], axis=1)
    lower = jnp.stack([-sine, cosine], axis=1)
    return jnp.stack([upper, lower], axis=0)


def section_two(first, second, direction):
    length = first * second
    outer = jnp.arange(first, dtype=jnp.int32)[:, None, None]
    inner = jnp.arange(second, dtype=jnp.int32)[None, :, None]
    final = jnp.arange(second, dtype=jnp.int32)[None, None, :]
    phase = (outer * inner + first * inner * final) % length
    angles = direction * 2.0 * math.pi / length * phase.astype(F32)
    cosine = jnp.cos(angles)
    sine = jnp.sin(angles)
    upper = jnp.stack([cosine, sine], axis=2)
    lower = jnp.stack([-sine, cosine], axis=2)
    return jnp.stack([upper, lower], axis=0)


def factored_transform(spectrum, direction):
    _, length, columns = spectrum.shape
    first, second = factor_pair(length)
    shaped = spectrum.reshape(2, first, second, columns)
    section = product("rabm,rask->skbm", shaped, section_one(length=first, direction=direction))
    result = product("skbm,skbtj->tjkm", section, section_two(first, second, direction))
    return result.reshape(2, length, columns)


def chan_forward(rows, channels, blocks):
    if channels <= DENSE_LIMIT:
        table = chan_table(channels, blocks)
        high, low = two_parts(table)
        rows_high, rows_low = split(rows)
        return dot(high, rows_high) + dot(high, rows_low) + dot(low, rows_high)
    columns = rows.shape[1]
    shaped = rows.reshape(blocks, 2, channels // blocks, columns).transpose(1, 0, 2, 3)
    return factored_transform(shaped.reshape(2, channels, columns), -1.0).reshape(2 * channels, columns)


def chan_inverse(rows, channels, blocks):
    if channels <= DENSE_LIMIT:
        high, low = two_parts(chan_table(channels, blocks))
        rows_high, rows_low = split(rows)
        back = ((0,), (0,))
        return dot(high, rows_high, back) + dot(high, rows_low, back) + dot(low, rows_high, back)
    columns = rows.shape[1]
    shaped = factored_transform(rows.reshape(2, channels, columns), 1.0)
    shaped = shaped.reshape(2, blocks, channels // blocks, columns).transpose(1, 0, 2, 3)
    return shaped.reshape(2 * channels, columns)


def time_forward_kernel(image_ref, high_ref, low_ref, out_ref):
    image = image_ref[...]
    rows = ((1,), (1,))
    out_ref[0] = dot(image, high_ref[...], rows) + dot(image, low_ref[...], rows)


def time_forward(image, high, low, cols):
    rows, samples = image.shape
    steps = samples // cols
    return pl.pallas_call(
        time_forward_kernel,
        grid=(steps,),
        in_specs=[
            pl.BlockSpec((rows, samples), lambda i: (0, 0)),
            pl.BlockSpec((cols, samples), lambda i: (i, 0)),
            pl.BlockSpec((cols, samples), lambda i: (i, 0)),
        ],
        out_specs=pl.BlockSpec((1, rows, cols), lambda i: (i, 0, 0)),
        out_shape=jax.ShapeDtypeStruct((steps, rows, cols), F32),
        cost_estimate=pl.CostEstimate(
            flops=4 * rows * samples * samples, bytes_accessed=4 * samples * samples, transcendentals=0
        ),
        compiler_params=pltpu.CompilerParams(vmem_limit_bytes=32 * 1024 * 1024),
    )(image, high, low)


def reduce_kernel(
    part_ref, out_ref, from_core, pair_sum, from_chip, win_sum, from_chan,
    core_send, core_recv, chip_send, chip_recv, chan_send, chan_recv,
):
    chan = lax.axis_index("chan")
    win = lax.axis_index("win")
    core = lax.rem(win, 2)
    chip = win // 2
    cols = out_ref.shape[1]
    core_peer = chip * 2 + 1 - core
    chip_peer = (1 - chip) * 2 + core
    barrier = pltpu.get_barrier_semaphore()
    mesh_ids = pl.DeviceIdType.MESH
    for peer in (core_peer, chip_peer):
        pl.semaphore_signal(barrier, inc=1, device_id={"win": peer}, device_id_type=mesh_ids)
    for step in range(1, 4):
        pl.semaphore_signal(barrier, inc=1, device_id={"chan": lax.rem(chan + step, 4)}, device_id_type=mesh_ids)
    pl.semaphore_wait(barrier, 5)

    def block(index):
        return pl.ds(pl.multiple_of(index * cols, 128), cols)

    core_copies = []
    for step in range(4):
        row = lax.rem(chan + 1 + step, 4)
        for side in range(2):
            copy = pltpu.make_async_remote_copy(
                src_ref=part_ref.at[row, :, block(2 * side + 1 - core)],
                dst_ref=from_core.at[step, side],
                send_sem=core_send.at[step, side],
                recv_sem=core_recv.at[step, side],
                device_id={"win": core_peer},
                device_id_type=mesh_ids,
            )
            copy.start()
            core_copies.append(copy)
    chip_copies = []
    for step in range(4):
        row = lax.rem(chan + 1 + step, 4)
        for side in range(2):
            core_copies[2 * step + side].wait()
            pair_sum[step, side] = part_ref[row, :, block(2 * side + core)] + from_core[step, side]
        copy = pltpu.make_async_remote_copy(
            src_ref=pair_sum.at[step, 1 - chip],
            dst_ref=from_chip.at[step],
            send_sem=chip_send.at[step],
            recv_sem=chip_recv.at[step],
            device_id={"win": chip_peer},
            device_id_type=mesh_ids,
        )
        copy.start()
        chip_copies.append(copy)
    chan_copies = []
    for step in range(4):
        chip_copies[step].wait()
        win_sum[step] = pair_sum[step, chip] + from_chip[step]
        if step < 3:
            copy = pltpu.make_async_remote_copy(
                src_ref=win_sum.at[step],
                dst_ref=from_chan.at[step],
                send_sem=chan_send.at[step],
                recv_sem=chan_recv.at[step],
                device_id={"chan": lax.rem(chan + 1 + step, 4)},
                device_id_type=mesh_ids,
            )
            copy.start()
            chan_copies.append(copy)
    for copy in chan_copies:
        copy.wait()
    out_ref[...] = win_sum[3] + from_chan[0] + from_chan[1] + from_chan[2]


def reduce_scatter(part):
    rows, columns = part.shape[0] // 4, part.shape[1] // 4
    piece = (rows, columns)
    dma = pltpu.SemaphoreType.DMA
    return pl.pallas_call(
        reduce_kernel,
        in_specs=[pl.BlockSpec(memory_space=pltpu.VMEM)],
        out_specs=pl.BlockSpec(memory_space=pltpu.VMEM),
        out_shape=jax.ShapeDtypeStruct(piece, F32),
        scratch_shapes=[
            pltpu.VMEM((4, 2) + piece, F32),
            pltpu.VMEM((4, 2) + piece, F32),
            pltpu.VMEM((4,) + piece, F32),
            pltpu.VMEM((4,) + piece, F32),
            pltpu.VMEM((3,) + piece, F32),
            dma((4, 2)),
            dma((4, 2)),
            dma((4,)),
            dma((4,)),
            dma((3,)),
            dma((3,)),
        ],
        compiler_params=pltpu.CompilerParams(
            collective_id=0, has_side_effects=True, vmem_limit_bytes=32 * 1024 * 1024
        ),
    )(part.reshape((4, rows, 4 * columns)))


def per_device(tokens, head_weight, target, target_amp, patch_ranks):
    blocks = lax.axis_size("chan")
    all_windows = lax.axis_size("win")
    tokens, target, target_amp, patch_ranks = tokens[0], target[0], target_amp[0], patch_ranks[0]
    local_patches, width = tokens.shape
    rows, samples = target.shape
    channels = rows * blocks
    half = samples // 2
    cols = half // blocks
    chan_patches = rows // PATCH_C
    sample_patches = samples // PATCH_S
    keep_count = local_patches * blocks // 4
    norm = 1.0 / math.sqrt(channels * samples)
    here = lax.axis_index("chan")

    upper = dot(target_amp[:, half:], negation(half))
    amp = jnp.stack([target_amp[:, :half].astype(F32), upper])
    amp = amp.reshape(2, rows, blocks, cols).transpose(2, 0, 1, 3)
    amp = lax.all_to_all(amp, "chan", split_axis=0, concat_axis=0, tiled=True)

    patches = dot(tokens, head_weight).astype(BF16)
    image = patches.reshape(chan_patches, sample_patches, PATCH_C, PATCH_S)
    image = image.transpose(0, 2, 1, 3).reshape(rows, samples)
    masked = (patch_ranks >= keep_count).reshape(chan_patches, 1, sample_patches, 1)
    pixel_mask = jnp.broadcast_to(masked, (chan_patches, PATCH_C, sample_patches, PATCH_S)).reshape(rows, samples)
    composite = jnp.where(pixel_mask, image, target)

    high, low = two_parts(time_table(samples, blocks))
    spectrum = time_forward(composite, high, low, cols).reshape(blocks, 2, rows, cols)
    spectrum = lax.all_to_all(spectrum, "chan", split_axis=0, concat_axis=0, tiled=True)

    lane = lax.broadcasted_iota(jnp.int32, (1, 128), 1)
    first_col = spectrum[:, :, :, :1]
    extra = jnp.where(lane == 0, first_col[:, 0], 0.0) + jnp.where(lane == 1, first_col[:, 1], 0.0)
    extra = jnp.stack([extra, jnp.zeros_like(extra)], axis=1)
    stacked = jnp.concatenate([spectrum, extra], axis=3).reshape(2 * channels, cols + 128)
    amp_low = amp[:, 0].reshape(channels, cols)
    amp_up = amp[:, 1].reshape(channels, cols)
    amp_sum = amp_low + dot(negation(channels).astype(F32), amp_up)
    amp_extra = jnp.where(lane == 0, amp_low[:, :1], amp_up[:, :1])
    amp_all = jnp.concatenate([amp_sum, amp_extra], axis=1)

    freq = chan_forward(stacked, channels, blocks).reshape(2, channels, cols + 128) * norm
    inverse_amp = lax.rsqrt(freq[0] * freq[0] + freq[1] * freq[1] + 1.0)
    scaled = freq * (inverse_amp * amp_all * norm)
    back = chan_inverse(scaled.reshape(2 * channels, cols + 128), channels, blocks)
    back = back.reshape(blocks, 2, rows, cols + 128)
    edge = jnp.stack([back[:, 0, :, cols : cols + 1], back[:, 0, :, cols + 1 : cols + 2]], axis=1)
    column = lax.broadcasted_iota(jnp.int32, (1, 1, 1, cols), 3)
    returned = jnp.where((column == 0) & (here == 0), edge, back[:, :, :, :cols])
    returned = lax.all_to_all(returned, "chan", split_axis=0, concat_axis=0, tiled=True)

    returned = returned.transpose(2, 0, 1, 3).reshape(rows, samples)
    returned_high, returned_low = split(returned)
    pulled = dot(returned_high, high) + dot(returned_low, high)
    grad_image = jnp.where(pixel_mask, (composite.astype(F32) - pulled) * (1.0 / all_windows), 0.0)
    grad_patches = grad_image.astype(BF16).reshape(chan_patches, PATCH_C, sample_patches, PATCH_S)
    grad_patches = grad_patches.transpose(0, 2, 1, 3).reshape(local_patches, PATCH_C * PATCH_S)
    grad_tokens = dot(grad_patches, head_weight, ((1,), (1,))).astype(BF16)
    grad_weight = dot(tokens, grad_patches, ((0,), (0,)))
    if all_windows == 4 and blocks == 4:
        grad_weight = reduce_scatter(grad_weight)
    else:
        grad_weight = lax.psum_scatter(grad_weight, "win", scatter_dimension=1, tiled=True)
        grad_weight = lax.psum_scatter(grad_weight, "chan", scatter_dimension=0, tiled=True)
    return (grad_tokens[None], grad_weight)


def solution(mesh):
    in_specs = (
        P(("groups", "win"), "chan", None),
        P(),
        P(("groups", "win"), "chan", None),
        P(("groups", "win"), "chan", None),
        P(("groups", "win"), "chan"),
    )
    out_specs = (P(("groups", "win"), "chan", None), P(("groups", "chan"), "win"))
    return jax.shard_map(
        per_device, mesh=mesh, in_specs=in_specs, out_specs=out_specs, check_vma=False
    )
```

```python
from functools import partial
import math

import jax
import jax.numpy as jnp
import numpy as np
from jax import lax
from jax.experimental import pallas as pl
from jax.experimental.pallas import tpu as pltpu
from jax.sharding import PartitionSpec as P

PATCH_C = 16
PATCH_S = 64
DENSE_LIMIT = 1024
F32 = jnp.float32
BF16 = jnp.bfloat16

product = partial(jnp.einsum, precision=lax.Precision.HIGHEST)


def two_parts(table):
    high = table.astype(BF16)
    low = (table - high.astype(np.float64)).astype(BF16)
    return high, low


def time_table(samples, blocks):
    half = samples // 2
    freq = np.arange(half)[:, None] * np.arange(samples)[None, :] % samples
    angles = 2.0 * np.pi / samples * freq
    cosine = np.cos(angles)
    sine = -np.sin(angles)
    sine[0] = 1.0 - 2.0 * (np.arange(samples) % 2)
    both = np.stack([cosine.reshape(blocks, -1, samples), sine.reshape(blocks, -1, samples)], axis=1)
    return both.reshape(samples, samples)


def chan_table(channels, blocks):
    angles = 2.0 * np.pi / channels * (np.arange(channels)[:, None] * np.arange(channels)[None, :] % channels)
    cosine = np.cos(angles)
    sine = np.sin(angles)
    table = np.stack([np.stack([cosine, sine], axis=1), np.stack([-sine, cosine], axis=1)], axis=0)
    table = table.reshape(2 * channels, 2, blocks, channels // blocks).transpose(0, 2, 1, 3)
    return table.reshape(2 * channels, 2 * channels)


def negation(length):
    table = np.zeros((length, length), np.float32)
    table[np.arange(length), -np.arange(length) % length] = 1.0
    return table.astype(BF16)


def dot(left, right, dims=((1,), (0,))):
    return lax.dot_general(left, right, (dims, ((), ())), preferred_element_type=F32)


def split(values):
    high = values.astype(BF16)
    return high, (values - high.astype(F32)).astype(BF16)


def factor_pair(length):
    first = int(math.isqrt(length))
    while length % first:
        first -= 1
    return (first, length // first)


def section_one(length, direction):
    index = jnp.arange(length, dtype=jnp.int32)
    angles = direction * 2.0 * math.pi / length * (index[:, None] * index[None, :] % length).astype(F32)
    cosine = jnp.cos(angles)
    sine = jnp.sin(angles)
    upper = jnp.stack([cosine, sine], axis=1)
    lower = jnp.stack([-sine, cosine], axis=1)
    return jnp.stack([upper, lower], axis=0)


def section_two(first, second, direction):
    length = first * second
    outer = jnp.arange(first, dtype=jnp.int32)[:, None, None]
    inner = jnp.arange(second, dtype=jnp.int32)[None, :, None]
    final = jnp.arange(second, dtype=jnp.int32)[None, None, :]
    phase = (outer * inner + first * inner * final) % length
    angles = direction * 2.0 * math.pi / length * phase.astype(F32)
    cosine = jnp.cos(angles)
    sine = jnp.sin(angles)
    upper = jnp.stack([cosine, sine], axis=2)
    lower = jnp.stack([-sine, cosine], axis=2)
    return jnp.stack([upper, lower], axis=0)


def factored_transform(spectrum, direction):
    _, length, columns = spectrum.shape
    first, second = factor_pair(length)
    shaped = spectrum.reshape(2, first, second, columns)
    section = product("rabm,rask->skbm", shaped, section_one(length=first, direction=direction))
    result = product("skbm,skbtj->tjkm", section, section_two(first, second, direction))
    return result.reshape(2, length, columns)


def chan_forward(rows, channels, blocks):
    if channels <= DENSE_LIMIT:
        table = chan_table(channels, blocks)
        high, low = two_parts(table)
        rows_high, rows_low = split(rows)
        return dot(high, rows_high) + dot(high, rows_low) + dot(low, rows_high)
    columns = rows.shape[1]
    shaped = rows.reshape(blocks, 2, channels // blocks, columns).transpose(1, 0, 2, 3)
    return factored_transform(shaped.reshape(2, channels, columns), -1.0).reshape(2 * channels, columns)


def chan_inverse(rows, channels, blocks):
    if channels <= DENSE_LIMIT:
        high, low = two_parts(chan_table(channels, blocks))
        rows_high, rows_low = split(rows)
        back = ((0,), (0,))
        return dot(high, rows_high, back) + dot(high, rows_low, back) + dot(low, rows_high, back)
    columns = rows.shape[1]
    shaped = factored_transform(rows.reshape(2, channels, columns), 1.0)
    shaped = shaped.reshape(2, blocks, channels // blocks, columns).transpose(1, 0, 2, 3)
    return shaped.reshape(2 * channels, columns)


def time_forward_kernel(image_ref, high_ref, low_ref, out_ref):
    image = image_ref[...]
    rows = ((1,), (1,))
    out_ref[0] = dot(image, high_ref[...], rows) + dot(image, low_ref[...], rows)


def time_forward(image, high, low, cols):
    rows, samples = image.shape
    steps = samples // cols
    return pl.pallas_call(
        time_forward_kernel,
        grid=(steps,),
        in_specs=[
            pl.BlockSpec((rows, samples), lambda i: (0, 0)),
            pl.BlockSpec((cols, samples), lambda i: (i, 0)),
            pl.BlockSpec((cols, samples), lambda i: (i, 0)),
        ],
        out_specs=pl.BlockSpec((1, rows, cols), lambda i: (i, 0, 0)),
        out_shape=jax.ShapeDtypeStruct((steps, rows, cols), F32),
        cost_estimate=pl.CostEstimate(
            flops=4 * rows * samples * samples, bytes_accessed=4 * samples * samples, transcendentals=0
        ),
        compiler_params=pltpu.CompilerParams(vmem_limit_bytes=32 * 1024 * 1024),
    )(image, high, low)


def reduce_kernel(
    part_ref, out_ref, from_core, pair_sum, from_chip, win_sum, from_chan,
    core_send, core_recv, chip_send, chip_recv, chan_send, chan_recv,
):
    chan = lax.axis_index("chan")
    win = lax.axis_index("win")
    core = lax.rem(win, 2)
    chip = win // 2
    cols = out_ref.shape[1]
    core_peer = chip * 2 + 1 - core
    chip_peer = (1 - chip) * 2 + core
    barrier = pltpu.get_barrier_semaphore()
    mesh_ids = pl.DeviceIdType.MESH
    for peer in (core_peer, chip_peer):
        pl.semaphore_signal(barrier, inc=1, device_id={"win": peer}, device_id_type=mesh_ids)
    for step in range(1, 4):
        pl.semaphore_signal(barrier, inc=1, device_id={"chan": lax.rem(chan + step, 4)}, device_id_type=mesh_ids)
    pl.semaphore_wait(barrier, 5)

    def block(index):
        return pl.ds(pl.multiple_of(index * cols, 128), cols)

    core_copies = []
    for step in range(4):
        row = lax.rem(chan + 1 + step, 4)
        for side in range(2):
            copy = pltpu.make_async_remote_copy(
                src_ref=part_ref.at[row, :, block(2 * side + 1 - core)],
                dst_ref=from_core.at[step, side],
                send_sem=core_send.at[step, side],
                recv_sem=core_recv.at[step, side],
                device_id={"win": core_peer},
                device_id_type=mesh_ids,
            )
            copy.start()
            core_copies.append(copy)
    chip_copies = []
    for step in range(4):
        row = lax.rem(chan + 1 + step, 4)
        for side in range(2):
            core_copies[2 * step + side].wait()
            pair_sum[step, side] = part_ref[row, :, block(2 * side + core)] + from_core[step, side]
        copy = pltpu.make_async_remote_copy(
            src_ref=pair_sum.at[step, 1 - chip],
            dst_ref=from_chip.at[step],
            send_sem=chip_send.at[step],
            recv_sem=chip_recv.at[step],
            device_id={"win": chip_peer},
            device_id_type=mesh_ids,
        )
        copy.start()
        chip_copies.append(copy)
    chan_copies = []
    for step in range(4):
        chip_copies[step].wait()
        win_sum[step] = pair_sum[step, chip] + from_chip[step]
        if step < 3:
            copy = pltpu.make_async_remote_copy(
                src_ref=win_sum.at[step],
                dst_ref=from_chan.at[step],
                send_sem=chan_send.at[step],
                recv_sem=chan_recv.at[step],
                device_id={"chan": lax.rem(chan + 1 + step, 4)},
                device_id_type=mesh_ids,
            )
            copy.start()
            chan_copies.append(copy)
    for copy in chan_copies:
        copy.wait()
    out_ref[...] = win_sum[3] + from_chan[0] + from_chan[1] + from_chan[2]


def reduce_scatter(part):
    rows, columns = part.shape[0] // 4, part.shape[1] // 4
    piece = (rows, columns)
    dma = pltpu.SemaphoreType.DMA
    return pl.pallas_call(
        reduce_kernel,
        in_specs=[pl.BlockSpec(memory_space=pltpu.VMEM)],
        out_specs=pl.BlockSpec(memory_space=pltpu.VMEM),
        out_shape=jax.ShapeDtypeStruct(piece, F32),
        scratch_shapes=[
            pltpu.VMEM((4, 2) + piece, F32),
            pltpu.VMEM((4, 2) + piece, F32),
            pltpu.VMEM((4,) + piece, F32),
            pltpu.VMEM((4,) + piece, F32),
            pltpu.VMEM((3,) + piece, F32),
            dma((4, 2)),
            dma((4, 2)),
            dma((4,)),
            dma((4,)),
            dma((3,)),
            dma((3,)),
        ],
        compiler_params=pltpu.CompilerParams(
            collective_id=0, has_side_effects=True, vmem_limit_bytes=32 * 1024 * 1024
        ),
    )(part.reshape((4, rows, 4 * columns)))


def per_device(tokens, head_weight, target, target_amp, patch_ranks):
    blocks = lax.axis_size("chan")
    all_windows = lax.axis_size("win")
    tokens, target, target_amp, patch_ranks = tokens[0], target[0], target_amp[0], patch_ranks[0]
    local_patches, width = tokens.shape
    rows, samples = target.shape
    channels = rows * blocks
    half = samples // 2
    cols = half // blocks
    chan_patches = rows // PATCH_C
    sample_patches = samples // PATCH_S
    keep_count = local_patches * blocks // 4
    norm = 1.0 / math.sqrt(channels * samples)
    here = lax.axis_index("chan")

    upper = dot(target_amp[:, half:], negation(half))
    amp = jnp.stack([target_amp[:, :half].astype(F32), upper])
    amp = amp.reshape(2, rows, blocks, cols).transpose(2, 0, 1, 3)
    amp = lax.all_to_all(amp, "chan", split_axis=0, concat_axis=0, tiled=True)

    patches = dot(tokens, head_weight).astype(BF16)
    image = patches.reshape(chan_patches, sample_patches, PATCH_C, PATCH_S)
    image = image.transpose(0, 2, 1, 3).reshape(rows, samples)
    masked = (patch_ranks >= keep_count).reshape(chan_patches, 1, sample_patches, 1)
    pixel_mask = jnp.broadcast_to(masked, (chan_patches, PATCH_C, sample_patches, PATCH_S)).reshape(rows, samples)
    composite = jnp.where(pixel_mask, image, target)

    high, low = two_parts(time_table(samples, blocks))
    spectrum = time_forward(composite, high, low, cols).reshape(blocks, 2, rows, cols)
    spectrum, amp = lax.optimization_barrier((spectrum, amp))
    spectrum = lax.all_to_all(spectrum, "chan", split_axis=0, concat_axis=0, tiled=True)

    lane = lax.broadcasted_iota(jnp.int32, (1, 128), 1)
    first_col = spectrum[:, :, :, :1]
    extra = jnp.where(lane == 0, first_col[:, 0], 0.0) + jnp.where(lane == 1, first_col[:, 1], 0.0)
    extra = jnp.stack([extra, jnp.zeros_like(extra)], axis=1)
    stacked = jnp.concatenate([spectrum, extra], axis=3).reshape(2 * channels, cols + 128)
    amp_low = amp[:, 0].reshape(channels, cols)
    amp_up = amp[:, 1].reshape(channels, cols)
    amp_sum = amp_low + dot(negation(channels).astype(F32), amp_up)
    amp_extra = jnp.where(lane == 0, amp_low[:, :1], amp_up[:, :1])
    amp_all = jnp.concatenate([amp_sum, amp_extra], axis=1)

    freq = chan_forward(stacked, channels, blocks).reshape(2, channels, cols + 128) * norm
    inverse_amp = lax.rsqrt(freq[0] * freq[0] + freq[1] * freq[1] + 1.0)
    scaled = freq * (inverse_amp * amp_all * norm)
    back = chan_inverse(scaled.reshape(2 * channels, cols + 128), channels, blocks)
    back = back.reshape(blocks, 2, rows, cols + 128)
    edge = jnp.stack([back[:, 0, :, cols : cols + 1], back[:, 0, :, cols + 1 : cols + 2]], axis=1)
    column = lax.broadcasted_iota(jnp.int32, (1, 1, 1, cols), 3)
    returned = jnp.where((column == 0) & (here == 0), edge, back[:, :, :, :cols])
    returned = lax.all_to_all(returned, "chan", split_axis=0, concat_axis=0, tiled=True)

    returned = returned.transpose(2, 0, 1, 3).reshape(rows, samples)
    returned_high, returned_low = split(returned)
    pulled = dot(returned_high, high) + dot(returned_low, high)
    grad_image = jnp.where(pixel_mask, (composite.astype(F32) - pulled) * (1.0 / all_windows), 0.0)
    grad_patches = grad_image.astype(BF16).reshape(chan_patches, PATCH_C, sample_patches, PATCH_S)
    grad_patches = grad_patches.transpose(0, 2, 1, 3).reshape(local_patches, PATCH_C * PATCH_S)
    grad_tokens = dot(grad_patches, head_weight, ((1,), (1,))).astype(BF16)
    grad_weight = dot(tokens, grad_patches, ((0,), (0,)))
    if all_windows == 4 and blocks == 4:
        grad_weight = reduce_scatter(grad_weight)
    else:
        grad_weight = lax.psum_scatter(grad_weight, "win", scatter_dimension=1, tiled=True)
        grad_weight = lax.psum_scatter(grad_weight, "chan", scatter_dimension=0, tiled=True)
    return (grad_tokens[None], grad_weight)


def solution(mesh):
    in_specs = (
        P(("groups", "win"), "chan", None),
        P(),
        P(("groups", "win"), "chan", None),
        P(("groups", "win"), "chan", None),
        P(("groups", "win"), "chan"),
    )
    out_specs = (P(("groups", "win"), "chan", None), P(("groups", "chan"), "win"))
    return jax.shard_map(
        per_device, mesh=mesh, in_specs=in_specs, out_specs=out_specs, check_vma=False
    )
```

```python
from functools import partial
import math

import jax
import jax.numpy as jnp
import numpy as np
from jax import lax
from jax.experimental import pallas as pl
from jax.experimental.pallas import tpu as pltpu
from jax.sharding import PartitionSpec as P

PATCH_C = 16
PATCH_S = 64
DENSE_LIMIT = 1024
F32 = jnp.float32
BF16 = jnp.bfloat16

product = partial(jnp.einsum, precision=lax.Precision.HIGHEST)


def two_parts(table):
    high = table.astype(BF16)
    low = (table - high.astype(np.float64)).astype(BF16)
    return high, low


def time_table(samples, blocks):
    half = samples // 2
    freq = np.arange(half)[:, None] * np.arange(samples)[None, :] % samples
    angles = 2.0 * np.pi / samples * freq
    cosine = np.cos(angles)
    sine = -np.sin(angles)
    sine[0] = 1.0 - 2.0 * (np.arange(samples) % 2)
    both = np.stack([cosine.reshape(blocks, -1, samples), sine.reshape(blocks, -1, samples)], axis=1)
    return both.reshape(samples, samples)


def chan_table(channels, blocks):
    angles = 2.0 * np.pi / channels * (np.arange(channels)[:, None] * np.arange(channels)[None, :] % channels)
    cosine = np.cos(angles)
    sine = np.sin(angles)
    table = np.stack([np.stack([cosine, sine], axis=1), np.stack([-sine, cosine], axis=1)], axis=0)
    table = table.reshape(2 * channels, 2, blocks, channels // blocks).transpose(0, 2, 1, 3)
    return table.reshape(2 * channels, 2 * channels)


def negation(length):
    table = np.zeros((length, length), np.float32)
    table[np.arange(length), -np.arange(length) % length] = 1.0
    return table.astype(BF16)


def dot(left, right, dims=((1,), (0,))):
    return lax.dot_general(left, right, (dims, ((), ())), preferred_element_type=F32)


def split(values):
    high = values.astype(BF16)
    return high, (values - high.astype(F32)).astype(BF16)


def factor_pair(length):
    first = int(math.isqrt(length))
    while length % first:
        first -= 1
    return (first, length // first)


def section_one(length, direction):
    index = jnp.arange(length, dtype=jnp.int32)
    angles = direction * 2.0 * math.pi / length * (index[:, None] * index[None, :] % length).astype(F32)
    cosine = jnp.cos(angles)
    sine = jnp.sin(angles)
    upper = jnp.stack([cosine, sine], axis=1)
    lower = jnp.stack([-sine, cosine], axis=1)
    return jnp.stack([upper, lower], axis=0)


def section_two(first, second, direction):
    length = first * second
    outer = jnp.arange(first, dtype=jnp.int32)[:, None, None]
    inner = jnp.arange(second, dtype=jnp.int32)[None, :, None]
    final = jnp.arange(second, dtype=jnp.int32)[None, None, :]
    phase = (outer * inner + first * inner * final) % length
    angles = direction * 2.0 * math.pi / length * phase.astype(F32)
    cosine = jnp.cos(angles)
    sine = jnp.sin(angles)
    upper = jnp.stack([cosine, sine], axis=2)
    lower = jnp.stack([-sine, cosine], axis=2)
    return jnp.stack([upper, lower], axis=0)


def factored_transform(spectrum, direction):
    _, length, columns = spectrum.shape
    first, second = factor_pair(length)
    shaped = spectrum.reshape(2, first, second, columns)
    section = product("rabm,rask->skbm", shaped, section_one(length=first, direction=direction))
    result = product("skbm,skbtj->tjkm", section, section_two(first, second, direction))
    return result.reshape(2, length, columns)


def chan_forward(rows, channels, blocks):
    if channels <= DENSE_LIMIT:
        table = chan_table(channels, blocks)
        high, low = two_parts(table)
        rows_high, rows_low = split(rows)
        return dot(high, rows_high) + dot(high, rows_low) + dot(low, rows_high)
    columns = rows.shape[1]
    shaped = rows.reshape(blocks, 2, channels // blocks, columns).transpose(1, 0, 2, 3)
    return factored_transform(shaped.reshape(2, channels, columns), -1.0).reshape(2 * channels, columns)


def chan_inverse(rows, channels, blocks):
    if channels <= DENSE_LIMIT:
        high, low = two_parts(chan_table(channels, blocks))
        rows_high, rows_low = split(rows)
        back = ((0,), (0,))
        return dot(high, rows_high, back) + dot(high, rows_low, back) + dot(low, rows_high, back)
    columns = rows.shape[1]
    shaped = factored_transform(rows.reshape(2, channels, columns), 1.0)
    shaped = shaped.reshape(2, blocks, channels // blocks, columns).transpose(1, 0, 2, 3)
    return shaped.reshape(2 * channels, columns)


def time_forward_kernel(image_ref, high_ref, low_ref, out_ref):
    image = image_ref[...]
    rows = ((1,), (1,))
    out_ref[0] = dot(image, high_ref[...], rows) + dot(image, low_ref[...], rows)


def time_forward(image, high, low, cols):
    rows, samples = image.shape
    steps = samples // cols
    return pl.pallas_call(
        time_forward_kernel,
        grid=(steps,),
        in_specs=[
            pl.BlockSpec((rows, samples), lambda i: (0, 0)),
            pl.BlockSpec((cols, samples), lambda i: (i, 0)),
            pl.BlockSpec((cols, samples), lambda i: (i, 0)),
        ],
        out_specs=pl.BlockSpec((1, rows, cols), lambda i: (i, 0, 0)),
        out_shape=jax.ShapeDtypeStruct((steps, rows, cols), F32),
        cost_estimate=pl.CostEstimate(
            flops=4 * rows * samples * samples, bytes_accessed=4 * samples * samples, transcendentals=0
        ),
        compiler_params=pltpu.CompilerParams(vmem_limit_bytes=32 * 1024 * 1024),
    )(image, high, low)


def channel_kernel(
    here_ref, rows_ref, amp_ref, high_ref, low_ref, back_high_ref, back_low_ref, flip_ref, out_ref,
    in_high, in_low, freq, mid_high, mid_low, upper, *, norm,
):
    blocks, _, local, cols = amp_ref.shape
    channels = blocks * local
    lane = lax.broadcasted_iota(jnp.int32, (local, 128), 1)
    for d in range(blocks):
        real = pl.ds(2 * d * local, local)
        imag = pl.ds((2 * d + 1) * local, local)
        for part in (real, imag):
            in_high[part, :cols], in_low[part, :cols] = split(rows_ref[part, :])
        edges = jnp.where(lane == 0, rows_ref[real, :1], jnp.where(lane == 1, rows_ref[imag, :1], 0.0))
        in_high[real, cols:], in_low[real, cols:] = split(edges)
        in_high[imag, cols:] = jnp.zeros((local, 128), BF16)
        in_low[imag, cols:] = jnp.zeros((local, 128), BF16)
        upper[pl.ds(d * local, local), :] = amp_ref[d, 1].astype(BF16)

    def product_of(high, low, part, right_high, right_low):
        return (
            dot(high[part, :], right_high[...])
            + dot(high[part, :], right_low[...])
            + dot(low[part, :], right_high[...])
        )

    for tile in range(2 * blocks):
        part = pl.ds(tile * local, local)
        freq[part, :] = product_of(high_ref, low_ref, part, in_high, in_low) * norm
    for d in range(blocks):
        real = pl.ds(d * local, local)
        imag = pl.ds(channels + d * local, local)
        amp_sum = amp_ref[d, 0] + dot(flip_ref[real, :], upper[...])
        amp_edges = jnp.where(lane == 0, amp_ref[d, 0][:, :1], amp_ref[d, 1][:, :1])
        for lanes, amp in ((pl.ds(0, cols), amp_sum), (pl.ds(cols, 128), amp_edges)):
            freq_real = freq[real, lanes]
            freq_imag = freq[imag, lanes]
            gain = lax.rsqrt(freq_real * freq_real + freq_imag * freq_imag + 1.0) * amp * norm
            mid_high[real, lanes], mid_low[real, lanes] = split(freq_real * gain)
            mid_high[imag, lanes], mid_low[imag, lanes] = split(freq_imag * gain)
    column = lax.broadcasted_iota(jnp.int32, (local, cols), 1)
    first = (column + here_ref[0]) == 0
    for d in range(blocks):
        real = pl.ds(2 * d * local, local)
        imag = pl.ds((2 * d + 1) * local, local)
        back_real = product_of(back_high_ref, back_low_ref, real, mid_high, mid_low)
        back_imag = product_of(back_high_ref, back_low_ref, imag, mid_high, mid_low)
        out_ref[real, :] = jnp.where(first, back_real[:, cols : cols + 1], back_real[:, :cols])
        out_ref[imag, :] = jnp.where(first, back_real[:, cols + 1 : cols + 2], back_imag[:, :cols])


def channel_pass(here, rows, amp, norm):
    blocks, _, local, cols = amp.shape
    channels = blocks * local
    table = chan_table(channels, blocks)
    vmem = pl.BlockSpec(memory_space=pltpu.VMEM)
    wide = (2 * channels, cols + 128)
    return pl.pallas_call(
        partial(channel_kernel, norm=norm),
        in_specs=[pl.BlockSpec(memory_space=pltpu.SMEM)] + [vmem] * 7,
        out_specs=vmem,
        out_shape=jax.ShapeDtypeStruct((2 * channels, cols), F32),
        scratch_shapes=[
            pltpu.VMEM(wide, BF16),
            pltpu.VMEM(wide, BF16),
            pltpu.VMEM(wide, F32),
            pltpu.VMEM(wide, BF16),
            pltpu.VMEM(wide, BF16),
            pltpu.VMEM((channels, cols), BF16),
        ],
        compiler_params=pltpu.CompilerParams(vmem_limit_bytes=40 * 1024 * 1024),
    )(here.reshape(1), rows, amp, *two_parts(table), *two_parts(np.ascontiguousarray(table.T)), negation(channels))


def general_pass(here, spectrum, amp, norm):
    blocks, _, rows, cols = amp.shape
    channels = blocks * rows
    lane = lax.broadcasted_iota(jnp.int32, (1, 128), 1)
    first_col = spectrum[:, :, :, :1]
    extra = jnp.where(lane == 0, first_col[:, 0], 0.0) + jnp.where(lane == 1, first_col[:, 1], 0.0)
    extra = jnp.stack([extra, jnp.zeros_like(extra)], axis=1)
    stacked = jnp.concatenate([spectrum, extra], axis=3).reshape(2 * channels, cols + 128)
    amp_low = amp[:, 0].reshape(channels, cols)
    amp_up = amp[:, 1].reshape(channels, cols)
    amp_sum = amp_low + dot(negation(channels).astype(F32), amp_up)
    amp_extra = jnp.where(lane == 0, amp_low[:, :1], amp_up[:, :1])
    amp_all = jnp.concatenate([amp_sum, amp_extra], axis=1)

    freq = chan_forward(stacked, channels, blocks).reshape(2, channels, cols + 128) * norm
    inverse_amp = lax.rsqrt(freq[0] * freq[0] + freq[1] * freq[1] + 1.0)
    scaled = freq * (inverse_amp * amp_all * norm)
    back = chan_inverse(scaled.reshape(2 * channels, cols + 128), channels, blocks)
    back = back.reshape(blocks, 2, rows, cols + 128)
    edge = jnp.stack([back[:, 0, :, cols : cols + 1], back[:, 0, :, cols + 1 : cols + 2]], axis=1)
    column = lax.broadcasted_iota(jnp.int32, (1, 1, 1, cols), 3)
    return jnp.where((column == 0) & (here == 0), edge, back[:, :, :, :cols])


def reduce_kernel(
    part_ref, out_ref, from_core, pair_sum, from_chip, win_sum, from_chan,
    core_send, core_recv, chip_send, chip_recv, chan_send, chan_recv,
):
    chan = lax.axis_index("chan")
    win = lax.axis_index("win")
    core = lax.rem(win, 2)
    chip = win // 2
    cols = out_ref.shape[1]
    core_peer = chip * 2 + 1 - core
    chip_peer = (1 - chip) * 2 + core
    barrier = pltpu.get_barrier_semaphore()
    mesh_ids = pl.DeviceIdType.MESH
    for peer in (core_peer, chip_peer):
        pl.semaphore_signal(barrier, inc=1, device_id={"win": peer}, device_id_type=mesh_ids)
    for step in range(1, 4):
        pl.semaphore_signal(barrier, inc=1, device_id={"chan": lax.rem(chan + step, 4)}, device_id_type=mesh_ids)
    pl.semaphore_wait(barrier, 5)

    def block(index):
        return pl.ds(pl.multiple_of(index * cols, 128), cols)

    core_copies = []
    for step in range(4):
        row = lax.rem(chan + 1 + step, 4)
        for side in range(2):
            copy = pltpu.make_async_remote_copy(
                src_ref=part_ref.at[row, :, block(2 * side + 1 - core)],
                dst_ref=from_core.at[step, side],
                send_sem=core_send.at[step, side],
                recv_sem=core_recv.at[step, side],
                device_id={"win": core_peer},
                device_id_type=mesh_ids,
            )
            copy.start()
            core_copies.append(copy)
    chip_copies = []
    for step in range(4):
        row = lax.rem(chan + 1 + step, 4)
        for side in range(2):
            core_copies[2 * step + side].wait()
            pair_sum[step, side] = part_ref[row, :, block(2 * side + core)] + from_core[step, side]
        copy = pltpu.make_async_remote_copy(
            src_ref=pair_sum.at[step, 1 - chip],
            dst_ref=from_chip.at[step],
            send_sem=chip_send.at[step],
            recv_sem=chip_recv.at[step],
            device_id={"win": chip_peer},
            device_id_type=mesh_ids,
        )
        copy.start()
        chip_copies.append(copy)
    chan_copies = []
    for step in range(4):
        chip_copies[step].wait()
        win_sum[step] = pair_sum[step, chip] + from_chip[step]
        if step < 3:
            copy = pltpu.make_async_remote_copy(
                src_ref=win_sum.at[step],
                dst_ref=from_chan.at[step],
                send_sem=chan_send.at[step],
                recv_sem=chan_recv.at[step],
                device_id={"chan": lax.rem(chan + 1 + step, 4)},
                device_id_type=mesh_ids,
            )
            copy.start()
            chan_copies.append(copy)
    for copy in chan_copies:
        copy.wait()
    out_ref[...] = win_sum[3] + from_chan[0] + from_chan[1] + from_chan[2]


def reduce_scatter(part):
    rows, columns = part.shape[0] // 4, part.shape[1] // 4
    piece = (rows, columns)
    dma = pltpu.SemaphoreType.DMA
    return pl.pallas_call(
        reduce_kernel,
        in_specs=[pl.BlockSpec(memory_space=pltpu.VMEM)],
        out_specs=pl.BlockSpec(memory_space=pltpu.VMEM),
        out_shape=jax.ShapeDtypeStruct(piece, F32),
        scratch_shapes=[
            pltpu.VMEM((4, 2) + piece, F32),
            pltpu.VMEM((4, 2) + piece, F32),
            pltpu.VMEM((4,) + piece, F32),
            pltpu.VMEM((4,) + piece, F32),
            pltpu.VMEM((3,) + piece, F32),
            dma((4, 2)),
            dma((4, 2)),
            dma((4,)),
            dma((4,)),
            dma((3,)),
            dma((3,)),
        ],
        compiler_params=pltpu.CompilerParams(
            collective_id=0, has_side_effects=True, vmem_limit_bytes=32 * 1024 * 1024
        ),
    )(part.reshape((4, rows, 4 * columns)))


def per_device(tokens, head_weight, target, target_amp, patch_ranks):
    blocks = lax.axis_size("chan")
    all_windows = lax.axis_size("win")
    tokens, target, target_amp, patch_ranks = tokens[0], target[0], target_amp[0], patch_ranks[0]
    local_patches, width = tokens.shape
    rows, samples = target.shape
    channels = rows * blocks
    half = samples // 2
    cols = half // blocks
    chan_patches = rows // PATCH_C
    sample_patches = samples // PATCH_S
    keep_count = local_patches * blocks // 4
    norm = 1.0 / math.sqrt(channels * samples)
    here = lax.axis_index("chan")

    upper = dot(target_amp[:, half:], negation(half))
    amp = jnp.stack([target_amp[:, :half].astype(F32), upper])
    amp = amp.reshape(2, rows, blocks, cols).transpose(2, 0, 1, 3)
    amp = lax.all_to_all(amp, "chan", split_axis=0, concat_axis=0, tiled=True)

    patches = dot(tokens, head_weight).astype(BF16)
    image = patches.reshape(chan_patches, sample_patches, PATCH_C, PATCH_S)
    image = image.transpose(0, 2, 1, 3).reshape(rows, samples)
    masked = (patch_ranks >= keep_count).reshape(chan_patches, 1, sample_patches, 1)
    pixel_mask = jnp.broadcast_to(masked, (chan_patches, PATCH_C, sample_patches, PATCH_S)).reshape(rows, samples)
    composite = jnp.where(pixel_mask, image, target)

    high, low = two_parts(time_table(samples, blocks))
    spectrum = time_forward(composite, high, low, cols).reshape(blocks, 2, rows, cols)
    spectrum, amp = lax.optimization_barrier((spectrum, amp))
    spectrum = lax.all_to_all(spectrum, "chan", split_axis=0, concat_axis=0, tiled=True)

    if channels <= DENSE_LIMIT and cols % 128 == 0:
        returned = channel_pass(here, spectrum.reshape(2 * channels, cols), amp, norm)
        returned = returned.reshape(blocks, 2, rows, cols)
    else:
        returned = general_pass(here, spectrum, amp, norm)
    returned = lax.all_to_all(returned, "chan", split_axis=0, concat_axis=0, tiled=True)

    returned = returned.transpose(2, 0, 1, 3).reshape(rows, samples)
    returned_high, returned_low = split(returned)
    pulled = dot(returned_high, high) + dot(returned_low, high)
    grad_image = jnp.where(pixel_mask, (composite.astype(F32) - pulled) * (1.0 / all_windows), 0.0)
    grad_patches = grad_image.astype(BF16).reshape(chan_patches, PATCH_C, sample_patches, PATCH_S)
    grad_patches = grad_patches.transpose(0, 2, 1, 3).reshape(local_patches, PATCH_C * PATCH_S)
    grad_tokens = dot(grad_patches, head_weight, ((1,), (1,))).astype(BF16)
    grad_weight = dot(tokens, grad_patches, ((0,), (0,)))
    if all_windows == 4 and blocks == 4:
        grad_weight = reduce_scatter(grad_weight)
    else:
        grad_weight = lax.psum_scatter(grad_weight, "win", scatter_dimension=1, tiled=True)
        grad_weight = lax.psum_scatter(grad_weight, "chan", scatter_dimension=0, tiled=True)
    return (grad_tokens[None], grad_weight)


def solution(mesh):
    in_specs = (
        P(("groups", "win"), "chan", None),
        P(),
        P(("groups", "win"), "chan", None),
        P(("groups", "win"), "chan", None),
        P(("groups", "win"), "chan"),
    )
    out_specs = (P(("groups", "win"), "chan", None), P(("groups", "chan"), "win"))
    return jax.shard_map(
        per_device, mesh=mesh, in_specs=in_specs, out_specs=out_specs, check_vma=False
    )
```

```python
from functools import partial
import math

import jax
import jax.numpy as jnp
import numpy as np
from jax import lax
from jax.experimental import pallas as pl
from jax.experimental.pallas import tpu as pltpu
from jax.sharding import PartitionSpec as P

PATCH_C = 16
PATCH_S = 64
DENSE_LIMIT = 1024
F32 = jnp.float32
BF16 = jnp.bfloat16

product = partial(jnp.einsum, precision=lax.Precision.HIGHEST)


def two_parts(table):
    high = table.astype(BF16)
    low = (table - high.astype(np.float64)).astype(BF16)
    return high, low


def time_table(samples, blocks):
    half = samples // 2
    freq = np.arange(half)[:, None] * np.arange(samples)[None, :] % samples
    angles = 2.0 * np.pi / samples * freq
    cosine = np.cos(angles)
    sine = -np.sin(angles)
    sine[0] = 1.0 - 2.0 * (np.arange(samples) % 2)
    both = np.stack([cosine.reshape(blocks, -1, samples), sine.reshape(blocks, -1, samples)], axis=1)
    return both.reshape(samples, samples)


def chan_table(channels, blocks):
    angles = 2.0 * np.pi / channels * (np.arange(channels)[:, None] * np.arange(channels)[None, :] % channels)
    cosine = np.cos(angles)
    sine = np.sin(angles)
    table = np.stack([np.stack([cosine, sine], axis=1), np.stack([-sine, cosine], axis=1)], axis=0)
    table = table.reshape(2 * channels, 2, blocks, channels // blocks).transpose(0, 2, 1, 3)
    return table.reshape(2 * channels, 2 * channels)


def negation(length):
    table = np.zeros((length, length), np.float32)
    table[np.arange(length), -np.arange(length) % length] = 1.0
    return table.astype(BF16)


def dot(left, right, dims=((1,), (0,))):
    return lax.dot_general(left, right, (dims, ((), ())), preferred_element_type=F32)


def split(values):
    high = values.astype(BF16)
    return high, (values - high.astype(F32)).astype(BF16)


def factor_pair(length):
    first = int(math.isqrt(length))
    while length % first:
        first -= 1
    return (first, length // first)


def section_one(length, direction):
    index = jnp.arange(length, dtype=jnp.int32)
    angles = direction * 2.0 * math.pi / length * (index[:, None] * index[None, :] % length).astype(F32)
    cosine = jnp.cos(angles)
    sine = jnp.sin(angles)
    upper = jnp.stack([cosine, sine], axis=1)
    lower = jnp.stack([-sine, cosine], axis=1)
    return jnp.stack([upper, lower], axis=0)


def section_two(first, second, direction):
    length = first * second
    outer = jnp.arange(first, dtype=jnp.int32)[:, None, None]
    inner = jnp.arange(second, dtype=jnp.int32)[None, :, None]
    final = jnp.arange(second, dtype=jnp.int32)[None, None, :]
    phase = (outer * inner + first * inner * final) % length
    angles = direction * 2.0 * math.pi / length * phase.astype(F32)
    cosine = jnp.cos(angles)
    sine = jnp.sin(angles)
    upper = jnp.stack([cosine, sine], axis=2)
    lower = jnp.stack([-sine, cosine], axis=2)
    return jnp.stack([upper, lower], axis=0)


def factored_transform(spectrum, direction):
    _, length, columns = spectrum.shape
    first, second = factor_pair(length)
    shaped = spectrum.reshape(2, first, second, columns)
    section = product("rabm,rask->skbm", shaped, section_one(length=first, direction=direction))
    result = product("skbm,skbtj->tjkm", section, section_two(first, second, direction))
    return result.reshape(2, length, columns)


def chan_forward(rows, channels, blocks):
    if channels <= DENSE_LIMIT:
        table = chan_table(channels, blocks)
        high, low = two_parts(table)
        rows_high, rows_low = split(rows)
        return dot(high, rows_high) + dot(high, rows_low) + dot(low, rows_high)
    columns = rows.shape[1]
    shaped = rows.reshape(blocks, 2, channels // blocks, columns).transpose(1, 0, 2, 3)
    return factored_transform(shaped.reshape(2, channels, columns), -1.0).reshape(2 * channels, columns)


def chan_inverse(rows, channels, blocks):
    if channels <= DENSE_LIMIT:
        high, low = two_parts(chan_table(channels, blocks))
        rows_high, rows_low = split(rows)
        back = ((0,), (0,))
        return dot(high, rows_high, back) + dot(high, rows_low, back) + dot(low, rows_high, back)
    columns = rows.shape[1]
    shaped = factored_transform(rows.reshape(2, channels, columns), 1.0)
    shaped = shaped.reshape(2, blocks, channels // blocks, columns).transpose(1, 0, 2, 3)
    return shaped.reshape(2 * channels, columns)


def time_forward_kernel(image_ref, high_ref, low_ref, out_ref):
    image = image_ref[...]
    rows = ((1,), (1,))
    out_ref[0] = dot(image, high_ref[...], rows) + dot(image, low_ref[...], rows)


def time_forward(image, high, low, cols):
    rows, samples = image.shape
    steps = samples // cols
    return pl.pallas_call(
        time_forward_kernel,
        grid=(steps,),
        in_specs=[
            pl.BlockSpec((rows, samples), lambda i: (0, 0)),
            pl.BlockSpec((cols, samples), lambda i: (i, 0)),
            pl.BlockSpec((cols, samples), lambda i: (i, 0)),
        ],
        out_specs=pl.BlockSpec((1, rows, cols), lambda i: (i, 0, 0)),
        out_shape=jax.ShapeDtypeStruct((steps, rows, cols), F32),
        cost_estimate=pl.CostEstimate(
            flops=4 * rows * samples * samples, bytes_accessed=4 * samples * samples, transcendentals=0
        ),
        compiler_params=pltpu.CompilerParams(vmem_limit_bytes=32 * 1024 * 1024),
    )(image, high, low)


def channel_kernel(
    here_ref, rows_ref, amp_ref, high_ref, low_ref, flip_ref, out_ref,
    in_high, in_low, freq, mid_high, mid_low, upper, *, norm,
):
    blocks, _, local, cols = amp_ref.shape
    channels = blocks * local
    lane = lax.broadcasted_iota(jnp.int32, (local, 128), 1)
    for d in range(blocks):
        real = pl.ds(2 * d * local, local)
        imag = pl.ds((2 * d + 1) * local, local)
        for part in (real, imag):
            in_high[part, :cols], in_low[part, :cols] = split(rows_ref[part, :])
        edges = jnp.where(lane == 0, rows_ref[real, :1], jnp.where(lane == 1, rows_ref[imag, :1], 0.0))
        in_high[real, cols:], in_low[real, cols:] = split(edges)
        in_high[imag, cols:] = jnp.zeros((local, 128), BF16)
        in_low[imag, cols:] = jnp.zeros((local, 128), BF16)
        upper[pl.ds(d * local, local), :] = amp_ref[d, 1].astype(BF16)

    for tile in range(2 * blocks):
        part = pl.ds(tile * local, local)
        table = high_ref[part, :]
        total = dot(table, in_high[...]) + dot(table, in_low[...]) + dot(low_ref[part, :], in_high[...])
        freq[part, :] = total * norm
    for d in range(blocks):
        real = pl.ds(d * local, local)
        imag = pl.ds(channels + d * local, local)
        amp_sum = amp_ref[d, 0] + dot(flip_ref[real, :], upper[...])
        amp_edges = jnp.where(lane == 0, amp_ref[d, 0][:, :1], amp_ref[d, 1][:, :1])
        for lanes, amp in ((pl.ds(0, cols), amp_sum), (pl.ds(cols, 128), amp_edges)):
            freq_real = freq[real, lanes]
            freq_imag = freq[imag, lanes]
            gain = lax.rsqrt(freq_real * freq_real + freq_imag * freq_imag + 1.0) * amp * norm
            mid_high[real, lanes], mid_low[real, lanes] = split(freq_real * gain)
            mid_high[imag, lanes], mid_low[imag, lanes] = split(freq_imag * gain)
    column = lax.broadcasted_iota(jnp.int32, (local, cols), 1)
    first = (column + here_ref[0]) == 0
    for d in range(blocks):
        real = pl.ds(2 * d * local, local)
        imag = pl.ds((2 * d + 1) * local, local)
        down = ((0,), (0,))
        back_real = dot(high_ref[:, real], mid_high[...], down) + dot(high_ref[:, real], mid_low[...], down)
        back_imag = dot(high_ref[:, imag], mid_high[...], down) + dot(high_ref[:, imag], mid_low[...], down)
        out_ref[real, :] = jnp.where(first, back_real[:, cols : cols + 1], back_real[:, :cols])
        out_ref[imag, :] = jnp.where(first, back_real[:, cols + 1 : cols + 2], back_imag[:, :cols])


def channel_pass(here, rows, amp, norm):
    blocks, _, local, cols = amp.shape
    channels = blocks * local
    table = chan_table(channels, blocks)
    vmem = pl.BlockSpec(memory_space=pltpu.VMEM)
    wide = (2 * channels, cols + 128)
    return pl.pallas_call(
        partial(channel_kernel, norm=norm),
        in_specs=[pl.BlockSpec(memory_space=pltpu.SMEM)] + [vmem] * 5,
        out_specs=vmem,
        out_shape=jax.ShapeDtypeStruct((2 * channels, cols), F32),
        scratch_shapes=[
            pltpu.VMEM(wide, BF16),
            pltpu.VMEM(wide, BF16),
            pltpu.VMEM(wide, F32),
            pltpu.VMEM(wide, BF16),
            pltpu.VMEM(wide, BF16),
            pltpu.VMEM((channels, cols), BF16),
        ],
        compiler_params=pltpu.CompilerParams(vmem_limit_bytes=40 * 1024 * 1024),
    )(here.reshape(1), rows, amp, *two_parts(table), negation(channels))


def amp_kernel(lower_ref, upper_ref, flip_ref, out_ref):
    out_ref[0, 0] = lower_ref[...].astype(F32)
    out_ref[0, 1] = dot(upper_ref[...], flip_ref[...])


def amp_blocks(target_amp, blocks):
    rows, samples = target_amp.shape
    half = samples // 2
    cols = half // blocks
    return pl.pallas_call(
        amp_kernel,
        grid=(blocks,),
        in_specs=[
            pl.BlockSpec((rows, cols), lambda i: (0, i)),
            pl.BlockSpec((rows, half), lambda i: (0, 1)),
            pl.BlockSpec((half, cols), lambda i: (0, i)),
        ],
        out_specs=pl.BlockSpec((1, 2, rows, cols), lambda i: (i, 0, 0, 0)),
        out_shape=jax.ShapeDtypeStruct((blocks, 2, rows, cols), F32),
    )(target_amp, target_amp, negation(half))


def general_pass(here, spectrum, amp, norm):
    blocks, _, rows, cols = amp.shape
    channels = blocks * rows
    lane = lax.broadcasted_iota(jnp.int32, (1, 128), 1)
    first_col = spectrum[:, :, :, :1]
    extra = jnp.where(lane == 0, first_col[:, 0], 0.0) + jnp.where(lane == 1, first_col[:, 1], 0.0)
    extra = jnp.stack([extra, jnp.zeros_like(extra)], axis=1)
    stacked = jnp.concatenate([spectrum, extra], axis=3).reshape(2 * channels, cols + 128)
    amp_low = amp[:, 0].reshape(channels, cols)
    amp_up = amp[:, 1].reshape(channels, cols)
    amp_sum = amp_low + dot(negation(channels).astype(F32), amp_up)
    amp_extra = jnp.where(lane == 0, amp_low[:, :1], amp_up[:, :1])
    amp_all = jnp.concatenate([amp_sum, amp_extra], axis=1)

    freq = chan_forward(stacked, channels, blocks).reshape(2, channels, cols + 128) * norm
    inverse_amp = lax.rsqrt(freq[0] * freq[0] + freq[1] * freq[1] + 1.0)
    scaled = freq * (inverse_amp * amp_all * norm)
    back = chan_inverse(scaled.reshape(2 * channels, cols + 128), channels, blocks)
    back = back.reshape(blocks, 2, rows, cols + 128)
    edge = jnp.stack([back[:, 0, :, cols : cols + 1], back[:, 0, :, cols + 1 : cols + 2]], axis=1)
    column = lax.broadcasted_iota(jnp.int32, (1, 1, 1, cols), 3)
    return jnp.where((column == 0) & (here == 0), edge, back[:, :, :, :cols])


def reduce_kernel(
    part_ref, out_ref, from_core, pair_sum, from_chip, win_sum, from_chan,
    core_send, core_recv, chip_send, chip_recv, chan_send, chan_recv,
):
    chan = lax.axis_index("chan")
    win = lax.axis_index("win")
    core = lax.rem(win, 2)
    chip = win // 2
    cols = out_ref.shape[1]
    core_peer = chip * 2 + 1 - core
    chip_peer = (1 - chip) * 2 + core
    barrier = pltpu.get_barrier_semaphore()
    mesh_ids = pl.DeviceIdType.MESH
    for peer in (core_peer, chip_peer):
        pl.semaphore_signal(barrier, inc=1, device_id={"win": peer}, device_id_type=mesh_ids)
    for step in range(1, 4):
        pl.semaphore_signal(barrier, inc=1, device_id={"chan": lax.rem(chan + step, 4)}, device_id_type=mesh_ids)
    pl.semaphore_wait(barrier, 5)

    def block(index):
        return pl.ds(pl.multiple_of(index * cols, 128), cols)

    core_copies = []
    for step in range(4):
        row = lax.rem(chan + 1 + step, 4)
        for side in range(2):
            copy = pltpu.make_async_remote_copy(
                src_ref=part_ref.at[row, :, block(2 * side + 1 - core)],
                dst_ref=from_core.at[step, side],
                send_sem=core_send.at[step, side],
                recv_sem=core_recv.at[step, side],
                device_id={"win": core_peer},
                device_id_type=mesh_ids,
            )
            copy.start()
            core_copies.append(copy)
    chip_copies = []
    for step in range(4):
        row = lax.rem(chan + 1 + step, 4)
        for side in range(2):
            core_copies[2 * step + side].wait()
            pair_sum[step, side] = part_ref[row, :, block(2 * side + core)] + from_core[step, side]
        copy = pltpu.make_async_remote_copy(
            src_ref=pair_sum.at[step, 1 - chip],
            dst_ref=from_chip.at[step],
            send_sem=chip_send.at[step],
            recv_sem=chip_recv.at[step],
            device_id={"win": chip_peer},
            device_id_type=mesh_ids,
        )
        copy.start()
        chip_copies.append(copy)
    chan_copies = []
    for step in range(4):
        chip_copies[step].wait()
        win_sum[step] = pair_sum[step, chip] + from_chip[step]
        if step < 3:
            copy = pltpu.make_async_remote_copy(
                src_ref=win_sum.at[step],
                dst_ref=from_chan.at[step],
                send_sem=chan_send.at[step],
                recv_sem=chan_recv.at[step],
                device_id={"chan": lax.rem(chan + 1 + step, 4)},
                device_id_type=mesh_ids,
            )
            copy.start()
            chan_copies.append(copy)
    for copy in chan_copies:
        copy.wait()
    out_ref[...] = win_sum[3] + from_chan[0] + from_chan[1] + from_chan[2]


def reduce_scatter(part):
    rows, columns = part.shape[0] // 4, part.shape[1] // 4
    piece = (rows, columns)
    dma = pltpu.SemaphoreType.DMA
    return pl.pallas_call(
        reduce_kernel,
        in_specs=[pl.BlockSpec(memory_space=pltpu.VMEM)],
        out_specs=pl.BlockSpec(memory_space=pltpu.VMEM),
        out_shape=jax.ShapeDtypeStruct(piece, F32),
        scratch_shapes=[
            pltpu.VMEM((4, 2) + piece, F32),
            pltpu.VMEM((4, 2) + piece, F32),
            pltpu.VMEM((4,) + piece, F32),
            pltpu.VMEM((4,) + piece, F32),
            pltpu.VMEM((3,) + piece, F32),
            dma((4, 2)),
            dma((4, 2)),
            dma((4,)),
            dma((4,)),
            dma((3,)),
            dma((3,)),
        ],
        compiler_params=pltpu.CompilerParams(
            collective_id=0, has_side_effects=True, vmem_limit_bytes=32 * 1024 * 1024
        ),
    )(part.reshape((4, rows, 4 * columns)))


def per_device(tokens, head_weight, target, target_amp, patch_ranks):
    blocks = lax.axis_size("chan")
    all_windows = lax.axis_size("win")
    tokens, target, target_amp, patch_ranks = tokens[0], target[0], target_amp[0], patch_ranks[0]
    local_patches, width = tokens.shape
    rows, samples = target.shape
    channels = rows * blocks
    half = samples // 2
    cols = half // blocks
    chan_patches = rows // PATCH_C
    sample_patches = samples // PATCH_S
    keep_count = local_patches * blocks // 4
    norm = 1.0 / math.sqrt(channels * samples)
    here = lax.axis_index("chan")

    if cols % 128 == 0:
        amp = amp_blocks(target_amp, blocks)
    else:
        upper = dot(target_amp[:, half:], negation(half))
        amp = jnp.stack([target_amp[:, :half].astype(F32), upper])
        amp = amp.reshape(2, rows, blocks, cols).transpose(2, 0, 1, 3)
    amp = lax.all_to_all(amp, "chan", split_axis=0, concat_axis=0, tiled=True)

    patches = dot(tokens, head_weight).astype(BF16)
    image = patches.reshape(chan_patches, sample_patches, PATCH_C, PATCH_S)
    image = image.transpose(0, 2, 1, 3).reshape(rows, samples)
    masked = (patch_ranks >= keep_count).reshape(chan_patches, 1, sample_patches, 1)
    pixel_mask = jnp.broadcast_to(masked, (chan_patches, PATCH_C, sample_patches, PATCH_S)).reshape(rows, samples)
    composite = jnp.where(pixel_mask, image, target)

    high, low = two_parts(time_table(samples, blocks))
    spectrum = time_forward(composite, high, low, cols).reshape(blocks, 2, rows, cols)
    spectrum, amp = lax.optimization_barrier((spectrum, amp))
    spectrum = lax.all_to_all(spectrum, "chan", split_axis=0, concat_axis=0, tiled=True)

    if channels <= DENSE_LIMIT and cols % 128 == 0:
        returned = channel_pass(here, spectrum.reshape(2 * channels, cols), amp, norm)
        returned = returned.reshape(blocks, 2, rows, cols)
    else:
        returned = general_pass(here, spectrum, amp, norm)
    returned = lax.all_to_all(returned, "chan", split_axis=0, concat_axis=0, tiled=True)

    returned = returned.transpose(2, 0, 1, 3).reshape(rows, samples)
    returned_high, returned_low = split(returned)
    pulled = dot(returned_high, high) + dot(returned_low, high)
    grad_image = jnp.where(pixel_mask, (composite.astype(F32) - pulled) * (1.0 / all_windows), 0.0)
    grad_patches = grad_image.astype(BF16).reshape(chan_patches, PATCH_C, sample_patches, PATCH_S)
    grad_patches = grad_patches.transpose(0, 2, 1, 3).reshape(local_patches, PATCH_C * PATCH_S)
    grad_tokens = dot(grad_patches, head_weight, ((1,), (1,))).astype(BF16)
    grad_weight = dot(tokens, grad_patches, ((0,), (0,)))
    if all_windows == 4 and blocks == 4:
        grad_weight = reduce_scatter(grad_weight)
    else:
        grad_weight = lax.psum_scatter(grad_weight, "win", scatter_dimension=1, tiled=True)
        grad_weight = lax.psum_scatter(grad_weight, "chan", scatter_dimension=0, tiled=True)
    return (grad_tokens[None], grad_weight)


def solution(mesh):
    in_specs = (
        P(("groups", "win"), "chan", None),
        P(),
        P(("groups", "win"), "chan", None),
        P(("groups", "win"), "chan", None),
        P(("groups", "win"), "chan"),
    )
    out_specs = (P(("groups", "win"), "chan", None), P(("groups", "chan"), "win"))
    return jax.shard_map(
        per_device, mesh=mesh, in_specs=in_specs, out_specs=out_specs, check_vma=False
    )
```
